256 devices in a mesh: row: 16 (over z, core), col: 4 (over y), depth: 4 (over x).
Axes of the slice: x: 4, y: 4, z: 8, core: 2. Of those that a mesh axis runs over, the one named last changes fastest.
Arguments:
- tokens: bfloat16 [1024, 8192], P(('col', 'depth'), 'row'), may hold values from -6 to 6
- out_grad: bfloat16 [1024, 8192], P(('col', 'depth'), 'row'), may hold values from -6 to 6
- gate_w: bfloat16 [8192, 14336], P('row', ('col', 'depth')), may hold values from -0.09375 to 0.09375
- up_w: bfloat16 [8192, 14336], P('row', ('col', 'depth')), may hold values from -0.09375 to 0.09375
- down_w: bfloat16 [14336, 8192], P(('col', 'depth'), 'row'), may hold values from -0.0625 to 0.0625
- keep_gate: int32 [64, 112], P('row', ('col', 'depth')), may hold values from 0 to 1, as said below
- keep_up: int32 [64, 112], P('row', ('col', 'depth')), may hold values from 0 to 1, as said below
- keep_down: int32 [112, 64], P(('col', 'depth'), 'row'), may hold values from 0 to 1, as said below
- exp_gate: int32 [64, 112], P('row', ('col', 'depth')), may hold values from -1 to 1
- exp_up: int32 [64, 112], P('row', ('col', 'depth')), may hold values from -1 to 1
- exp_down: int32 [112, 64], P(('col', 'depth'), 'row'), may hold values from -1 to 1
Outputs:
- output: bfloat16 [1024, 8192], P(('col', 'depth'), 'row')
- input_grad: bfloat16 [1024, 8192], P(('col', 'depth'), 'row')
- gate_w_grad: bfloat16 [8192, 14336], P('row', ('col', 'depth'))
- up_w_grad: bfloat16 [8192, 14336], P('row', ('col', 'depth'))
- down_w_grad: bfloat16 [14336, 8192], P(('col', 'depth'), 'row')
The draws below stay inside these ranges and needn't reach their ends.
Inputs may be any that keep to these rules, and one draw needn't show every extreme that they name: `keep_gate`: 1 where a weight block is kept, 0 where it is dropped; the share kept may differ from one block column to another. `keep_up`: 1 where a weight block is kept, 0 where it is dropped; the share kept may differ from one block column to another. `keep_down`: 1 where a weight block is kept, 0 where it is dropped; the share kept may differ from one block column to another.
All inputs are finite; a program needn't handle non-finite values.
Results may differ from the reference program's by a relative error of at most 0.005.
Values may be sent and summed in bfloat16 or wider, within the bound.
No kernel may reach another device: no remote copies, remote signals or barrier semaphores. Data moves between devices by JAX's collectives and lax.ppermute only.
A program may use at most 128 MiB of HBM per device.

```python
import jax
import jax.numpy as jnp

D = 8192
FF = 14336
BLOCK = 128
TOKENS = 1024


def draw_blocks(key, rows, cols):
    level = jax.random.randint(jax.random.fold_in(key, 11), (1, cols), 1, 4)
    coin = jax.random.randint(jax.random.fold_in(key, 23), (rows, cols), 0, 4)
    return (coin < level).astype(jnp.int32)


def draw_keep_gate(key, part):
    return draw_blocks(jax.random.fold_in(key, 101), D // BLOCK, FF // BLOCK)


def draw_keep_up(key, part):
    return draw_blocks(jax.random.fold_in(key, 202), D // BLOCK, FF // BLOCK)


def draw_keep_down(key, part):
    return draw_blocks(jax.random.fold_in(key, 303), FF // BLOCK, D // BLOCK)


def set_ends(drawn, stream_key, smallest, largest):
    longest = drawn.shape.index(max(drawn.shape))
    spots = []
    for shift in (0, 1):
        where = [jax.random.randint(jax.random.fold_in(stream_key, axis), (), 0, length) for axis, length in enumerate(drawn.shape)]
        where[longest] = (where[longest] + shift) % drawn.shape[longest]
        spots.append(tuple(where))
    return drawn.at[spots[0]].set(smallest).at[spots[1]].set(largest)


def block_levels(stream_key, shape, pieces, least, high):
    def one(axis_at, parts):
        steps = jax.random.uniform(jax.random.fold_in(jax.random.fold_in(stream_key, 6), axis_at), (parts,), jnp.float32, least / len(pieces), high / len(pieces))
        return jnp.repeat(jnp.exp(steps), shape[axis_at] // parts).reshape((-1,) + (1,) * (len(shape) - axis_at - 1))

    level = one(*pieces[0])
    for cut in pieces[1:]:
        level = level * one(*cut)
    return level


def noise(own_key, shape, spread, most, cuts=(), kind=jnp.bfloat16):
    drawn = jax.random.normal(own_key, shape, jnp.float32) * spread
    if len(cuts) > 0:
        drawn = block_levels(own_key, shape, cuts, -0.22, 0.18) * drawn
    return jnp.clip(drawn, min=-most, max=most).astype(kind)


def setup_inputs(seed: int = 0) -> dict:
    key_list = jax.random.split(jax.random.key(seed), 12)
    return {
        "tokens": noise(key_list[0], (TOKENS, D), 1.0, 6.0, ((0, 16), (1, 16))),
        "out_grad": noise(key_list[1], (TOKENS, D), 1.0, 6.0, ((0, 16), (1, 16))),
        "gate_w": noise(key_list[2], (D, FF), (D // 2) ** -0.5, 0.09375, ((0, 16), (1, 16))),
        "up_w": noise(key_list[3], (D, FF), (D // 2) ** -0.5, 0.09375, ((0, 16), (1, 16))),
        "down_w": noise(key_list[4], (FF, D), (FF // 2) ** -0.5, 0.0625, ((0, 16), (1, 16))),
        "keep_gate": draw_keep_gate(jax.random.fold_in(key_list[11], 71), 0),
        "keep_up": draw_keep_up(jax.random.fold_in(key_list[11], 71), 0),
        "keep_down": draw_keep_down(jax.random.fold_in(key_list[11], 71), 0),
        "exp_gate": set_ends(jax.random.randint(key_list[8], (D // BLOCK, FF // BLOCK), -1, 2), jax.random.fold_in(key_list[8], 1), -1, 1).astype(jnp.int32),
        "exp_up": set_ends(jax.random.randint(key_list[9], (D // BLOCK, FF // BLOCK), -1, 2), jax.random.fold_in(key_list[9], 1), -1, 1).astype(jnp.int32),
        "exp_down": set_ends(jax.random.randint(key_list[10], (FF // BLOCK, D // BLOCK), -1, 2), jax.random.fold_in(key_list[10], 1), -1, 1).astype(jnp.int32),
    }


def block_factor(keep, exps):
    return keep.astype(jnp.float32) * jnp.exp2(exps.astype(jnp.float32))

def scaled(raw, factor):
    rows, cols = factor.shape
    high = raw.shape[0] // rows
    wide = raw.shape[1] // cols
    blocks = raw.reshape(rows, high, cols, wide) * factor.astype(jnp.bfloat16)[:, None, :, None]
    return blocks.reshape(raw.shape)

def masked_grad(grad, factor):
    rows, cols = factor.shape
    blocks = grad.reshape(rows, grad.shape[0] // rows, cols, grad.shape[1] // cols) * factor[:, None, :, None]
    return blocks.reshape(grad.shape).astype(jnp.bfloat16)

def reference(tokens, out_grad, gate_w, up_w, down_w, keep_gate, keep_up, keep_down, exp_gate, exp_up, exp_down):
    factor_gate = block_factor(keep_gate, exp_gate)
    factor_up = block_factor(keep_up, exp_up)
    factor_down = block_factor(keep_down, exp_down)
    eff_gate = scaled(gate_w, factor_gate)
    eff_up = scaled(up_w, factor_up)
    eff_down = scaled(down_w, factor_down)
    gate = jnp.dot(tokens, eff_gate, preferred_element_type=jnp.float32)
    up = jnp.dot(tokens, eff_up, preferred_element_type=jnp.float32)
    hidden_grad = jnp.dot(out_grad, eff_down.T, preferred_element_type=jnp.float32)
    sig = jax.nn.sigmoid(gate)
    hidden = (gate * sig * up).astype(jnp.bfloat16)
    output = jnp.dot(hidden, eff_down, preferred_element_type=jnp.float32).astype(jnp.bfloat16)
    gate_grad = (hidden_grad * up * sig * (1.0 + gate * (1.0 - sig))).astype(jnp.bfloat16)
    up_grad = (hidden_grad * gate * sig).astype(jnp.bfloat16)
    input_grad = (jnp.dot(gate_grad, eff_gate.T, preferred_element_type=jnp.float32) + jnp.dot(up_grad, eff_up.T, preferred_element_type=jnp.float32)).astype(jnp.bfloat16)
    gate_w_grad = masked_grad(jnp.dot(tokens.T, gate_grad, preferred_element_type=jnp.float32), factor_gate)
    up_w_grad = masked_grad(jnp.dot(tokens.T, up_grad, preferred_element_type=jnp.float32), factor_up)
    down_w_grad = masked_grad(jnp.dot(hidden.T, out_grad, preferred_element_type=jnp.float32), factor_down)
    return (output, input_grad, gate_w_grad, up_w_grad, down_w_grad)
```

```python
import jax
import jax.numpy as jnp
from jax import lax
from jax.sharding import PartitionSpec as P

F32 = jnp.float32
BF16 = jnp.bfloat16
F16 = jnp.float16

PAIR_SCALE = 4.0
GRAD_SCALE = 8.0


def block_factor(keep, exps):
    return keep.astype(F32) * jnp.exp2(exps.astype(F32))


def scaled(raw, factor):
    rows, cols = factor.shape
    high = raw.shape[0] // rows
    wide = raw.shape[1] // cols
    blocks = raw.reshape(rows, high, cols, wide) * factor.astype(BF16)[:, None, :, None]
    return blocks.reshape(raw.shape)


def masked_grad(grad, factor):
    rows, cols = factor.shape
    blocks = (
        grad.reshape(rows, grad.shape[0] // rows, cols, grad.shape[1] // cols)
        * factor[:, None, :, None]
    )
    return blocks.reshape(grad.shape).astype(BF16)


def activate(gate, up, hidden_grad):
    sig = jax.nn.sigmoid(gate)
    hidden = (gate * sig * up).astype(BF16)
    gate_grad = (hidden_grad * up * sig * (1.0 + gate * (1.0 - sig))).astype(BF16)
    up_grad = (hidden_grad * gate * sig).astype(BF16)
    return (hidden, gate_grad, up_grad)


def shift(x, axis, n, k):
    return lax.ppermute(x, axis, [(i, (i + k) % n) for i in range(n)])


def zshift(x, k):
    return lax.ppermute(x, "row", [(i, (i + 2 * k) % 16) for i in range(16)])


def swap_core(x):
    return lax.ppermute(x, "row", [(i, i ^ 1) for i in range(16)])


def pick(x, index, axis=0):
    return lax.dynamic_index_in_dim(x, index, axis, keepdims=False)


def gather_first(block, first, second, me_first, me_second, first_is_major):
    rows, width = block.shape
    got = jnp.zeros((4, rows, width), block.dtype)
    got = lax.dynamic_update_index_in_dim(got, block, me_first, 0)
    for k in (1, 3, 2):
        got = lax.dynamic_update_index_in_dim(got, shift(block, first, 4, k), (me_first - k) % 4, 0)
    axis = 1 if first_is_major else 0
    shape = [4, rows, width]
    shape.insert(axis, 4)
    whole = jnp.zeros(shape, block.dtype)
    whole = lax.dynamic_update_index_in_dim(whole, got, me_second, axis)
    for k in (1, 3, 2):
        whole = lax.dynamic_update_index_in_dim(whole, shift(got, second, 4, k), (me_second - k) % 4, axis)
    return whole.reshape(16 * rows, width)


def add16(a, b):
    return (a.astype(F32) + b.astype(F32)).astype(F16)


def sum_over_row(term, z, core):
    width = term.shape[1]
    parts = term.reshape(8, 2, 64, width)
    mine = add16(pick(parts, core, 1), swap_core(pick(parts, 1 - core, 1)))
    ahead = pick(mine, (z + 4) % 8)
    back = pick(mine, (z - 3) % 8)
    for s in range(4):
        ahead = zshift(ahead, 1)
        if s < 3:
            ahead = add16(ahead, pick(mine, (z + 3 - s) % 8))
            back = zshift(back, -1)
            if s < 2:
                back = add16(back, pick(mine, (z - 2 + s) % 8))
    return pick(mine, z).astype(F32) + ahead.astype(F32) + back.astype(F32)


def shards(
    tokens,
    out_grad,
    gate_w,
    up_w,
    down_w,
    keep_gate,
    keep_up,
    keep_down,
    exp_gate,
    exp_up,
    exp_down,
):
    row = lax.axis_index("row")
    z, core = row // 2, row % 2
    col, depth = lax.axis_index("col"), lax.axis_index("depth")
    factor_gate = block_factor(keep_gate, exp_gate)
    factor_up = block_factor(keep_up, exp_up)
    factor_down = block_factor(keep_down, exp_down)
    eff_gate = scaled(gate_w, factor_gate)
    eff_up = scaled(up_w, factor_up)
    eff_down = scaled(down_w, factor_down)
    width = gate_w.shape[1]
    paired = jnp.concatenate([eff_gate, eff_up], axis=1)
    all_tokens = gather_first(tokens, "depth", "col", depth, col, False)
    all_grads = gather_first(out_grad, "col", "depth", col, depth, True)

    pair_term = (jnp.dot(all_tokens, paired, preferred_element_type=F32) * PAIR_SCALE).astype(F16)
    grad_term = (
        lax.dot_general(all_grads, eff_down, (((1,), (1,)), ((), ())), preferred_element_type=F32)
        * GRAD_SCALE
    ).astype(F16)
    pair = sum_over_row(pair_term, z, core) * (1.0 / PAIR_SCALE)
    hidden_grad = sum_over_row(grad_term, z, core) * (1.0 / GRAD_SCALE)
    acts = activate(pair[:, :width], pair[:, width:], hidden_grad)
    whole = lax.all_gather(jnp.concatenate(acts, axis=1), "row", axis=0, tiled=True)
    hidden_all = whole[:, :width]
    pair_grad = whole[:, width:]
    result = jnp.concatenate(
        [
            jnp.dot(hidden_all, eff_down, preferred_element_type=F32).astype(BF16),
            lax.dot_general(
                pair_grad, paired, (((1,), (1,)), ((), ())), preferred_element_type=F32
            ).astype(BF16),
        ],
        axis=1,
    )
    panel = down_w.shape[1]
    moved = lax.all_to_all(result, ("col", "depth"), 0, 0, tiled=True)
    sums = jnp.sum(moved.reshape(16, 64, 2 * panel).astype(F32), axis=0).astype(BF16)
    output = sums[:, :panel]
    input_grad = sums[:, panel:]
    tn = (((0,), (0,)), ((), ()))
    pair_weights = lax.dot_general(all_tokens, pair_grad, tn, preferred_element_type=F32)
    gate_w_grad = masked_grad(pair_weights[:, :width], factor_gate)
    up_w_grad = masked_grad(pair_weights[:, width:], factor_up)
    down_w_grad = masked_grad(
        lax.dot_general(hidden_all, all_grads, tn, preferred_element_type=F32), factor_down
    )
    return (output, input_grad, gate_w_grad, up_w_grad, down_w_grad)


def solution(mesh):
    act = P(("col", "depth"), "row")
    wide = P("row", ("col", "depth"))
    return jax.shard_map(
        shards,
        mesh=mesh,
        in_specs=(act, act, wide, wide, act, wide, wide, act, wide, wide, act),
        out_specs=(act, act, wide, wide, act),
        check_vma=False,
    )
```

```python
import jax
import jax.numpy as jnp
from jax import lax
from jax.experimental import pallas as pl
from jax.experimental.pallas import tpu as pltpu
from jax.sharding import PartitionSpec as P

F32 = jnp.float32
BF16 = jnp.bfloat16
F16 = jnp.float16
BLOCK = 128

PAIR_SCALE = 4.0
GRAD_SCALE = 8.0

NT = (((1,), (1,)), ((), ()))
TN = (((0,), (0,)), ((), ()))


def dot(a, b, dims=(((1,), (0,)), ((), ()))):
    return lax.dot_general(a, b, dims, preferred_element_type=F32)


def factor_of(keep, exps):
    return keep.astype(F32) * (jnp.left_shift(1, exps + 1).astype(F32) * 0.5)


def scale_kernel(kg, ku, kd, eg, eu, ed, gate, up, down, pair_out, down_out):
    i = pl.program_id(0)
    cols = gate.shape[1] // BLOCK
    for j in range(cols):
        at = pl.ds(j * BLOCK, BLOCK)
        pair_out[:, at] = gate[:, at] * factor_of(kg[i, j], eg[i, j]).astype(BF16)
        pair_out[:, pl.ds((cols + j) * BLOCK, BLOCK)] = up[:, at] * factor_of(ku[i, j], eu[i, j]).astype(BF16)
        down_out[at, :] = down[at, :] * factor_of(kd[j, i], ed[j, i]).astype(BF16)


def scale_weights(gate_w, up_w, down_w, keep_gate, keep_up, keep_down, exp_gate, exp_up, exp_down):
    panel, width = gate_w.shape
    smem = pl.BlockSpec(memory_space=pltpu.SMEM)
    wide = pl.BlockSpec((BLOCK, width), lambda i: (i, 0))
    tall = pl.BlockSpec((width, BLOCK), lambda i: (0, i))
    return pl.pallas_call(
        scale_kernel,
        grid=(panel // BLOCK,),
        in_specs=[smem] * 6 + [wide, wide, tall],
        out_specs=[pl.BlockSpec((BLOCK, 2 * width), lambda i: (i, 0)), tall],
        out_shape=[
            jax.ShapeDtypeStruct((panel, 2 * width), BF16),
            jax.ShapeDtypeStruct((width, panel), BF16),
        ],
        name="scale_weights",
    )(keep_gate, keep_up, keep_down, exp_gate, exp_up, exp_down, gate_w, up_w, down_w)


def spread(factor):
    rows, cols = factor.shape
    tall = (lax.broadcasted_iota(jnp.int32, (rows * BLOCK, rows), 0) // BLOCK
            == lax.broadcasted_iota(jnp.int32, (rows * BLOCK, rows), 1)).astype(BF16)
    wide = (lax.broadcasted_iota(jnp.int32, (cols, cols * BLOCK), 1) // BLOCK
            == lax.broadcasted_iota(jnp.int32, (cols, cols * BLOCK), 0)).astype(BF16)
    return dot(tall, dot(factor.astype(BF16), wide).astype(BF16)).astype(BF16)


def activate(gate, up, hidden_grad):
    sig = jax.nn.sigmoid(gate)
    hidden = (gate * sig * up).astype(BF16)
    gate_grad = (hidden_grad * up * sig * (1.0 + gate * (1.0 - sig))).astype(BF16)
    up_grad = (hidden_grad * gate * sig).astype(BF16)
    return (hidden, gate_grad, up_grad)


def shift(x, first, k):
    pairs = []
    for row in range(16):
        for col in range(4):
            for depth in range(4):
                if (row % 2 == 0) == first:
                    there = (row * 4 + col) * 4 + (depth + k) % 4
                else:
                    there = (row * 4 + (col + k) % 4) * 4 + depth
                pairs.append(((row * 4 + col) * 4 + depth, there))
    return lax.ppermute(x, ("row", "col", "depth"), pairs)


def zshift(x, k):
    return lax.ppermute(x, "row", [(i, (i + 2 * k) % 16) for i in range(16)])


def swap_core(x):
    return lax.ppermute(x, "row", [(i, i ^ 1) for i in range(16)])


def pick(x, index, axis=0):
    return lax.dynamic_index_in_dim(x, index, axis, keepdims=False)


def put(x, block, index, axis=0):
    return lax.dynamic_update_index_in_dim(x, block, index, axis)


def place(core, col, depth, k, j):
    along_depth = (col + j) % 4 * 4 + (depth + k) % 4
    along_col = (col + k) % 4 * 4 + (depth + j) % 4
    return jnp.where(core == 0, along_depth, along_col)


def gather_xy(block, core, col, depth):
    got = jnp.stack([block] + [shift(block, True, k) for k in range(1, 4)])
    whole = jnp.zeros((16, *block.shape), block.dtype)
    for j in (0, 1, 3, 2):
        came = got if j == 0 else shift(got, False, j)
        for k in range(4):
            whole = put(whole, came[k], place(core, col, depth, -k, -j))
    return whole.reshape(-1, block.shape[1])


def sum_over_xy(term, core, col, depth):
    width = term.shape[1]
    parts = term.reshape(16, -1, width)
    part = None
    for k in (1, 3, 2, 0):
        block = jnp.stack([pick(parts, place(core, col, depth, j, k)) for j in range(4)])
        block = (block if k == 0 else shift(block, False, k)).astype(F32)
        part = block if part is None else part + block
    part16 = part.astype(BF16)
    total = part[0]
    for j in (1, 3, 2):
        total += shift(part16[j], True, j).astype(F32)
    return total


def add16(a, b):
    return (a.astype(F32) + b.astype(F32)).astype(F16)


def sum_over_row(term, z, core):
    width = term.shape[1]
    parts = term.reshape(2, 8, -1, width)
    mine = add16(pick(parts, core), swap_core(pick(parts, 1 - core)))
    ahead = pick(mine, (z + 4) % 8)
    back = pick(mine, (z - 3) % 8)
    for s in range(4):
        ahead = zshift(ahead, 1)
        if s < 3:
            ahead = add16(ahead, pick(mine, (z + 3 - s) % 8))
            back = zshift(back, -1)
            if s < 2:
                back = add16(back, pick(mine, (z - 2 + s) % 8))
    return pick(mine, z).astype(F32) + ahead.astype(F32) + back.astype(F32)


def gather_row(block, z, core):
    rows, width = block.shape
    mine = put(jnp.zeros((8, rows, width), block.dtype), block, z)
    ahead, back = block, block
    for s in range(4):
        ahead = zshift(ahead, 1)
        mine = put(mine, ahead, (z - 1 - s) % 8)
        if s < 3:
            back = zshift(back, -1)
            mine = put(mine, back, (z + 1 + s) % 8)
    other = swap_core(mine)
    whole = put(put(jnp.zeros((2, 8, rows, width), block.dtype), mine, core), other, 1 - core)
    return whole.reshape(16 * rows, width)


def shards(
    tokens,
    out_grad,
    gate_w,
    up_w,
    down_w,
    keep_gate,
    keep_up,
    keep_down,
    exp_gate,
    exp_up,
    exp_down,
):
    row = lax.axis_index("row")
    z, core = row // 2, row % 2
    col, depth = lax.axis_index("col"), lax.axis_index("depth")
    width = gate_w.shape[1]
    panel = gate_w.shape[0]

    gathered = gather_xy(jnp.concatenate([tokens, out_grad], axis=1), core, col, depth)
    paired, eff_down = scale_weights(
        gate_w, up_w, down_w, keep_gate, keep_up, keep_down, exp_gate, exp_up, exp_down
    )
    all_tokens, all_grads = gathered[:, :panel], gathered[:, panel:]
    term = jnp.concatenate(
        [
            (dot(all_tokens, paired) * PAIR_SCALE).astype(F16),
            (dot(all_grads, eff_down, NT) * GRAD_SCALE).astype(F16),
        ],
        axis=1,
    )
    sums = sum_over_row(term, z, core)
    acts = activate(
        sums[:, :width] * (1.0 / PAIR_SCALE),
        sums[:, width : 2 * width] * (1.0 / PAIR_SCALE),
        sums[:, 2 * width :] * (1.0 / GRAD_SCALE),
    )
    whole = gather_row(jnp.concatenate(acts, axis=1), z, core)
    hidden_all, pair_grad = whole[:, :width], whole[:, width:]
    result = sum_over_xy(
        jnp.concatenate(
            [dot(hidden_all, eff_down).astype(BF16), dot(pair_grad, paired, NT).astype(BF16)], axis=1
        ),
        core,
        col,
        depth,
    ).astype(BF16)
    output, input_grad = result[:, :panel], result[:, panel:]

    down_w_grad = (
        dot(hidden_all, all_grads, TN) * spread(factor_of(keep_down, exp_down)).astype(F32)
    ).astype(BF16)
    gate_w_grad = (
        dot(all_tokens, pair_grad[:, :width], TN) * spread(factor_of(keep_gate, exp_gate)).astype(F32)
    ).astype(BF16)
    up_w_grad = (
        dot(all_tokens, pair_grad[:, width:], TN) * spread(factor_of(keep_up, exp_up)).astype(F32)
    ).astype(BF16)
    return (output, input_grad, gate_w_grad, up_w_grad, down_w_grad)


def solution(mesh):
    act = P(("col", "depth"), "row")
    wide = P("row", ("col", "depth"))
    return jax.shard_map(
        shards,
        mesh=mesh,
        in_specs=(act, act, wide, wide, act, wide, wide, act, wide, wide, act),
        out_specs=(act, act, wide, wide, act),
        check_vma=False,
    )
```

```python
import jax
import jax.numpy as jnp
from jax import lax
from jax.experimental import pallas as pl
from jax.experimental.pallas import tpu as pltpu
from jax.sharding import PartitionSpec as P

F32 = jnp.float32
BF16 = jnp.bfloat16
F16 = jnp.float16
BLOCK = 128
CHUNKS = 2

PAIR_SCALE = 4.0
GRAD_SCALE = 8.0

NT = (((1,), (1,)), ((), ()))
TN = (((0,), (0,)), ((), ()))


def dot(a, b, dims=(((1,), (0,)), ((), ()))):
    return lax.dot_general(a, b, dims, preferred_element_type=F32)


def factor_of(keep, exps):
    return keep.astype(F32) * (jnp.left_shift(1, exps + 1).astype(F32) * 0.5)


def scale_kernel(kg, ku, kd, eg, eu, ed, gate, up, down, pair_out, down_out):
    i = pl.program_id(0)
    cols = gate.shape[1] // BLOCK
    for j in range(cols):
        at = pl.ds(j * BLOCK, BLOCK)
        pair_out[:, at] = gate[:, at] * factor_of(kg[i, j], eg[i, j]).astype(BF16)
        pair_out[:, pl.ds((cols + j) * BLOCK, BLOCK)] = up[:, at] * factor_of(ku[i, j], eu[i, j]).astype(BF16)
        down_out[at, :] = down[at, :] * factor_of(kd[j, i], ed[j, i]).astype(BF16)


def scale_weights(gate_w, up_w, down_w, keep_gate, keep_up, keep_down, exp_gate, exp_up, exp_down):
    panel, width = gate_w.shape
    smem = pl.BlockSpec(memory_space=pltpu.SMEM)
    wide = pl.BlockSpec((BLOCK, width), lambda i: (i, 0))
    tall = pl.BlockSpec((width, BLOCK), lambda i: (0, i))
    return pl.pallas_call(
        scale_kernel,
        grid=(panel // BLOCK,),
        in_specs=[smem] * 6 + [wide, wide, tall],
        out_specs=[pl.BlockSpec((BLOCK, 2 * width), lambda i: (i, 0)), tall],
        out_shape=[
            jax.ShapeDtypeStruct((panel, 2 * width), BF16),
            jax.ShapeDtypeStruct((width, panel), BF16),
        ],
        name="scale_weights",
    )(keep_gate, keep_up, keep_down, exp_gate, exp_up, exp_down, gate_w, up_w, down_w)


def spread(factor):
    rows, cols = factor.shape
    tall = (lax.broadcasted_iota(jnp.int32, (rows * BLOCK, rows), 0) // BLOCK
            == lax.broadcasted_iota(jnp.int32, (rows * BLOCK, rows), 1)).astype(BF16)
    wide = (lax.broadcasted_iota(jnp.int32, (cols, cols * BLOCK), 1) // BLOCK
            == lax.broadcasted_iota(jnp.int32, (cols, cols * BLOCK), 0)).astype(BF16)
    return dot(tall, dot(factor.astype(BF16), wide).astype(BF16)).astype(BF16)


def activate(gate, up, hidden_grad):
    sig = jax.nn.sigmoid(gate)
    hidden = (gate * sig * up).astype(BF16)
    gate_grad = (hidden_grad * up * sig * (1.0 + gate * (1.0 - sig))).astype(BF16)
    up_grad = (hidden_grad * gate * sig).astype(BF16)
    return (hidden, gate_grad, up_grad)


def shift(x, first, k):
    pairs = []
    for row in range(16):
        for col in range(4):
            for depth in range(4):
                if (row % 2 == 0) == first:
                    there = (row * 4 + col) * 4 + (depth + k) % 4
                else:
                    there = (row * 4 + (col + k) % 4) * 4 + depth
                pairs.append(((row * 4 + col) * 4 + depth, there))
    return lax.ppermute(x, ("row", "col", "depth"), pairs)


def zshift(x, k):
    return lax.ppermute(x, "row", [(i, (i + 2 * k) % 16) for i in range(16)])


def swap_core(x):
    return lax.ppermute(x, "row", [(i, i ^ 1) for i in range(16)])


def pick(x, index, axis=0):
    return lax.dynamic_index_in_dim(x, index, axis, keepdims=False)


def put(x, block, index, axis=0):
    return lax.dynamic_update_index_in_dim(x, block, index, axis)


def place(core, col, depth, k, j):
    along_depth = (col + j) % 4 * 4 + (depth + k) % 4
    along_col = (col + k) % 4 * 4 + (depth + j) % 4
    return jnp.where(core == 0, along_depth, along_col)


def gather_xy(block, core, col, depth):
    got = jnp.stack([block] + [shift(block, True, k) for k in range(1, 4)])
    whole = jnp.zeros((16, *block.shape), block.dtype)
    for j in (0, 1, 3, 2):
        came = got if j == 0 else shift(got, False, j)
        for k in range(4):
            whole = put(whole, came[k], place(core, col, depth, -k, -j))
    return whole.reshape(-1, block.shape[1])


def sum_over_xy(term, core, col, depth):
    width = term.shape[1]
    parts = term.reshape(16, -1, width)
    part = None
    for k in (1, 3, 2, 0):
        block = jnp.stack([pick(parts, place(core, col, depth, j, k)) for j in range(4)])
        block = (block if k == 0 else shift(block, False, k)).astype(F32)
        part = block if part is None else part + block
    part16 = part.astype(BF16)
    total = part[0]
    for j in (1, 3, 2):
        total += shift(part16[j], True, j).astype(F32)
    return total


def add16(a, b):
    return (a.astype(F32) + b.astype(F32)).astype(F16)


def sum_over_row(term, z, core):
    width = term.shape[1]
    parts = term.reshape(2, 8, -1, width)
    mine = add16(pick(parts, core), swap_core(pick(parts, 1 - core)))
    ahead = pick(mine, (z + 4) % 8)
    back = pick(mine, (z - 3) % 8)
    for s in range(4):
        ahead = zshift(ahead, 1)
        if s < 3:
            ahead = add16(ahead, pick(mine, (z + 3 - s) % 8))
            back = zshift(back, -1)
            if s < 2:
                back = add16(back, pick(mine, (z - 2 + s) % 8))
    return pick(mine, z).astype(F32) + ahead.astype(F32) + back.astype(F32)


def gather_row(block, z, core):
    rows, width = block.shape
    mine = put(jnp.zeros((8, rows, width), block.dtype), block, z)
    ahead, back = block, block
    for s in range(4):
        ahead = zshift(ahead, 1)
        mine = put(mine, ahead, (z - 1 - s) % 8)
        if s < 3:
            back = zshift(back, -1)
            mine = put(mine, back, (z + 1 + s) % 8)
    other = swap_core(mine)
    whole = put(put(jnp.zeros((2, 8, rows, width), block.dtype), mine, core), other, 1 - core)
    return whole.reshape(16 * rows, width)


def shards(
    tokens,
    out_grad,
    gate_w,
    up_w,
    down_w,
    keep_gate,
    keep_up,
    keep_down,
    exp_gate,
    exp_up,
    exp_down,
):
    row = lax.axis_index("row")
    z, core = row // 2, row % 2
    col, depth = lax.axis_index("col"), lax.axis_index("depth")
    width = gate_w.shape[1]
    panel = gate_w.shape[0]

    paired, eff_down = scale_weights(
        gate_w, up_w, down_w, keep_gate, keep_up, keep_down, exp_gate, exp_up, exp_down
    )
    both = jnp.concatenate([tokens, out_grad], axis=1)
    half = both.shape[0] // CHUNKS
    gathered, whole, result = [], [], []
    for c in range(CHUNKS):
        inputs = gather_xy(both[c * half : (c + 1) * half], core, col, depth)
        term = jnp.concatenate(
            [
                (dot(inputs[:, :panel], paired) * PAIR_SCALE).astype(F16),
                (dot(inputs[:, panel:], eff_down, NT) * GRAD_SCALE).astype(F16),
            ],
            axis=1,
        )
        sums = sum_over_row(term, z, core)
        acts = activate(
            sums[:, :width] * (1.0 / PAIR_SCALE),
            sums[:, width : 2 * width] * (1.0 / PAIR_SCALE),
            sums[:, 2 * width :] * (1.0 / GRAD_SCALE),
        )
        hid = gather_row(jnp.concatenate(acts, axis=1), z, core)
        back = jnp.concatenate(
            [
                dot(hid[:, :width], eff_down).astype(BF16),
                dot(hid[:, width:], paired, NT).astype(BF16),
            ],
            axis=1,
        )
        result.append(sum_over_xy(back, core, col, depth).astype(BF16))
        gathered.append(inputs)
        whole.append(hid)
    result = jnp.concatenate(result)
    output, input_grad = result[:, :panel], result[:, panel:]
    gathered = jnp.concatenate(gathered)
    whole = jnp.concatenate(whole)
    all_tokens, all_grads = gathered[:, :panel], gathered[:, panel:]
    hidden_all, pair_grad = whole[:, :width], whole[:, width:]

    down_w_grad = (
        dot(hidden_all, all_grads, TN) * spread(factor_of(keep_down, exp_down)).astype(F32)
    ).astype(BF16)
    gate_w_grad = (
        dot(all_tokens, pair_grad[:, :width], TN) * spread(factor_of(keep_gate, exp_gate)).astype(F32)
    ).astype(BF16)
    up_w_grad = (
        dot(all_tokens, pair_grad[:, width:], TN) * spread(factor_of(keep_up, exp_up)).astype(F32)
    ).astype(BF16)
    return (output, input_grad, gate_w_grad, up_w_grad, down_w_grad)


def solution(mesh):
    act = P(("col", "depth"), "row")
    wide = P("row", ("col", "depth"))
    return jax.shard_map(
        shards,
        mesh=mesh,
        in_specs=(act, act, wide, wide, act, wide, wide, act, wide, wide, act),
        out_specs=(act, act, wide, wide, act),
        check_vma=False,
    )
```

```python
import jax
import jax.numpy as jnp
from jax import lax
from jax.experimental import pallas as pl
from jax.experimental.pallas import tpu as pltpu
from jax.sharding import PartitionSpec as P

F32 = jnp.float32
BF16 = jnp.bfloat16
F16 = jnp.float16
BLOCK = 128
STREAMS = 2

PAIR_SCALE = 4.0
GRAD_SCALE = 8.0

NT = (((1,), (1,)), ((), ()))
TN = (((0,), (0,)), ((), ()))


def dot(a, b, dims=(((1,), (0,)), ((), ()))):
    return lax.dot_general(a, b, dims, preferred_element_type=F32)


def factor_of(keep, exps):
    return keep.astype(F32) * (jnp.left_shift(1, exps + 1).astype(F32) * 0.5)


def scale_kernel(kg, ku, kd, eg, eu, ed, gate, up, down, pair_out, down_out, pair_mask, down_mask):
    i = pl.program_id(0)
    cols = gate.shape[1] // BLOCK
    for j in range(cols):
        at = pl.ds(j * BLOCK, BLOCK)
        there = pl.ds((cols + j) * BLOCK, BLOCK)
        gate_factor = jnp.full((BLOCK, BLOCK), factor_of(kg[i, j], eg[i, j]), F32).astype(BF16)
        up_factor = jnp.full((BLOCK, BLOCK), factor_of(ku[i, j], eu[i, j]), F32).astype(BF16)
        down_factor = jnp.full((BLOCK, BLOCK), factor_of(kd[i, j], ed[i, j]), F32).astype(BF16)
        pair_mask[:, at] = gate_factor
        pair_mask[:, there] = up_factor
        down_mask[at, :] = down_factor
        pair_out[:, at] = gate[:, at] * gate_factor
        pair_out[:, there] = up[:, at] * up_factor
        down_out[at, :] = down[at, :] * down_factor


def scale_weights(gate_w, up_w, down_w, keep_gate, keep_up, keep_down, exp_gate, exp_up, exp_down):
    panel, width = gate_w.shape
    smem = pl.BlockSpec(memory_space=pltpu.SMEM)
    wide = pl.BlockSpec((BLOCK, width), lambda i: (i, 0))
    pair = pl.BlockSpec((BLOCK, 2 * width), lambda i: (i, 0))
    tall = pl.BlockSpec((width, BLOCK), lambda i: (0, i))
    pair_shape = jax.ShapeDtypeStruct((panel, 2 * width), BF16)
    down_shape = jax.ShapeDtypeStruct((width, panel), BF16)
    return pl.pallas_call(
        scale_kernel,
        grid=(panel // BLOCK,),
        in_specs=[smem] * 6 + [wide, wide, tall],
        out_specs=[pair, tall, pair, tall],
        out_shape=[pair_shape, down_shape, pair_shape, down_shape],
        compiler_params=pltpu.CompilerParams(vmem_limit_bytes=6 * 2**20),
        name="scale_weights",
    )(keep_gate, keep_up, keep_down.T, exp_gate, exp_up, exp_down.T, gate_w, up_w, down_w)


def activate(gate, up, hidden_grad):
    sig = jax.nn.sigmoid(gate)
    hidden = (gate * sig * up).astype(BF16)
    gate_grad = (hidden_grad * up * sig * (1.0 + gate * (1.0 - sig))).astype(BF16)
    up_grad = (hidden_grad * gate * sig).astype(BF16)
    return (hidden, gate_grad, up_grad)


def shift(x, first, k):
    pairs = []
    for row in range(16):
        for col in range(4):
            for depth in range(4):
                if (row % 2 == 0) == first:
                    there = (row * 4 + col) * 4 + (depth + k) % 4
                else:
                    there = (row * 4 + (col + k) % 4) * 4 + depth
                pairs.append(((row * 4 + col) * 4 + depth, there))
    return lax.ppermute(x, ("row", "col", "depth"), pairs)


def zshift(x, k):
    return lax.ppermute(x, "row", [(i, (i + 2 * k) % 16) for i in range(16)])


def swap_core(x):
    return lax.ppermute(x, "row", [(i, i ^ 1) for i in range(16)])


def pick(x, index, axis=0):
    return lax.dynamic_index_in_dim(x, index, axis, keepdims=False)


def put(x, block, index, axis=0):
    return lax.dynamic_update_index_in_dim(x, block, index, axis)


def zero_after(x):
    x = lax.slice(x, (0,) * x.ndim, (1,) * x.ndim).reshape(())
    return (x != x).astype(jnp.int32)


def place(core, col, depth, k, j):
    along_depth = (col + j) % 4 * 4 + (depth + k) % 4
    along_col = (col + k) % 4 * 4 + (depth + j) % 4
    return jnp.where(core == 0, along_depth, along_col ^ 8)


def gather_xy_first(block):
    return [block] + [shift(block, True, k) for k in range(1, 4)]


def gather_xy_second(got, core, col, depth):
    block = got[0]
    got = jnp.stack(got)
    whole = jnp.zeros((16, *block.shape), block.dtype)
    for j in (0, 1, 3, 2):
        came = got if j == 0 else shift(got, False, j)
        for k in range(4):
            whole = put(whole, came[k], place(core, col, depth, -k, -j))
    return whole.reshape(-1, block.shape[1])


def sum_over_xy(term, core, col, depth):
    width = term.shape[1]
    parts = term.reshape(16, -1, width)
    part = None
    for k in (1, 3, 2, 0):
        block = jnp.stack([pick(parts, place(core, col, depth, j, k)) for j in range(4)])
        block = (block if k == 0 else shift(block, False, k)).astype(F32)
        part = block if part is None else part + block
    part16 = part.astype(BF16)
    total = part[0]
    for j in (1, 3, 2):
        total += shift(part16[j], True, j).astype(F32)
    return total


def sum_over_z(mine, z):
    ahead = mine((z + 4) % 8)
    back = mine((z - 3) % 8)
    for s in range(4):
        ahead = zshift(ahead, 1)
        if s < 3:
            ahead = add16(ahead, mine((z + 3 - s) % 8))
            back = zshift(back, -1)
            if s < 2:
                back = add16(back, mine((z - 2 + s) % 8))
    return mine(z).astype(F32) + ahead.astype(F32) + back.astype(F32)


def gather_z(block, z):
    rows, width = block.shape
    whole = put(jnp.zeros((8, rows, width), block.dtype), block, z)
    ahead, back = block, block
    for s in range(4):
        ahead = zshift(ahead, 1)
        whole = put(whole, ahead, (z - 1 - s) % 8)
        if s < 3:
            back = zshift(back, -1)
            whole = put(whole, back, (z + 1 + s) % 8)
    return whole.reshape(8 * rows, width)


def add16(a, b):
    return (a.astype(F32) + b.astype(F32)).astype(F16)


def back_kernel(*refs):
    *acts, pair, down, out = refs
    width, panel = down.shape
    rows = acts[0].shape[0]
    for i, act in enumerate(acts):
        at = pl.ds(i * rows, rows)
        out[at, pl.ds(0, panel)] = dot(act[:, pl.ds(0, width)], down[...]).astype(BF16)
        out[at, pl.ds(panel, panel)] = dot(act[:, pl.ds(width, 2 * width)], pair[...], NT).astype(BF16)


def back_terms(acts, paired, eff_down):
    panel = eff_down.shape[1]
    rows = sum(a.shape[0] for a in acts)
    flops = 2 * rows * panel * 3 * eff_down.shape[0]
    return pl.pallas_call(
        back_kernel,
        in_specs=[pl.BlockSpec(memory_space=pltpu.VMEM)] * (len(acts) + 2),
        out_specs=pl.BlockSpec(memory_space=pltpu.VMEM),
        out_shape=jax.ShapeDtypeStruct((rows, 2 * panel), BF16),
        cost_estimate=pl.CostEstimate(flops=flops, bytes_accessed=12 * 2**20, transcendentals=0),
        compiler_params=pltpu.CompilerParams(vmem_limit_bytes=14 * 2**20),
        name="back_terms",
    )(*acts, paired, eff_down)


def shards(
    tokens,
    out_grad,
    gate_w,
    up_w,
    down_w,
    keep_gate,
    keep_up,
    keep_down,
    exp_gate,
    exp_up,
    exp_down,
):
    row = lax.axis_index("row")
    z, core = row // 2, row % 2
    col, depth = lax.axis_index("col"), lax.axis_index("depth")
    width = gate_w.shape[1]
    panel = gate_w.shape[0]

    got = gather_xy_first(jnp.concatenate([tokens, out_grad], axis=1))
    paired, eff_down, pair_mask, down_mask = scale_weights(
        gate_w, up_w, down_w, keep_gate, keep_up, keep_down, exp_gate + zero_after(got[3]), exp_up, exp_down
    )
    gathered = gather_xy_second(got, core, col, depth)
    half = gathered.shape[0] // 2
    rows = half // STREAMS

    def pair_term(at):
        return dot(gathered[at : at + rows, :panel], paired) * PAIR_SCALE

    def grad_term(at):
        return dot(gathered[at : at + rows, panel:], eff_down, NT) * GRAD_SCALE

    came, acts = [], []
    for s in range(STREAMS):
        at = half + s * rows
        term = jnp.concatenate([pair_term(at).astype(F16), grad_term(at).astype(F16)], axis=1)
        came.append(swap_core(term))
    for s in range(STREAMS):
        mine_pair = (pair_term(s * rows) + came[s][:, : 2 * width].astype(F32)).astype(F16)
        mine_grad = (grad_term(s * rows) + came[s][:, 2 * width :].astype(F32)).astype(F16)
        mine_pair = mine_pair.reshape(8, -1, 2 * width)
        mine_grad = mine_grad.reshape(8, -1, width)

        def mine(at, a=mine_pair, b=mine_grad):
            return jnp.concatenate([pick(a, at), pick(b, at)], axis=1)

        sums = sum_over_z(mine, z)
        act = activate(
            sums[:, :width] * (1.0 / PAIR_SCALE),
            sums[:, width : 2 * width] * (1.0 / PAIR_SCALE),
            sums[:, 2 * width :] * (1.0 / GRAD_SCALE),
        )
        acts.append(gather_z(jnp.concatenate(act, axis=1), z))
    acts += [swap_core(a) for a in acts]
    result = sum_over_xy(back_terms(acts, paired, eff_down), core, col, depth).astype(BF16)
    output, input_grad = result[:, :panel], result[:, panel:]

    all_tokens, all_grads = gathered[:, :panel], gathered[:, panel:]
    whole = jnp.concatenate(acts)
    hidden_all, pair_grad = whole[:, :width], whole[:, width:]

    down_w_grad = (dot(hidden_all, all_grads, TN) * down_mask.astype(F32)).astype(BF16)
    gate_w_grad = (
        dot(all_tokens, pair_grad[:, :width], TN) * pair_mask[:, :width].astype(F32)
    ).astype(BF16)
    up_w_grad = (
        dot(all_tokens, pair_grad[:, width:], TN) * pair_mask[:, width:].astype(F32)
    ).astype(BF16)
    return (output, input_grad, gate_w_grad, up_w_grad, down_w_grad)


def solution(mesh):
    act = P(("col", "depth"), "row")
    wide = P("row", ("col", "depth"))
    return jax.shard_map(
        shards,
        mesh=mesh,
        in_specs=(act, act, wide, wide, act, wide, wide, act, wide, wide, act),
        out_specs=(act, act, wide, wide, act),
        check_vma=False,
    )
```

```python
import jax
import jax.numpy as jnp
from jax import lax
from jax.experimental import pallas as pl
from jax.experimental.pallas import tpu as pltpu
from jax.sharding import PartitionSpec as P

F32 = jnp.float32
BF16 = jnp.bfloat16
F16 = jnp.float16
BLOCK = 128
STREAMS = 2

PAIR_SCALE = 4.0
GRAD_SCALE = 8.0

NT = (((1,), (1,)), ((), ()))
TN = (((0,), (0,)), ((), ()))


def dot(a, b, dims=(((1,), (0,)), ((), ()))):
    return lax.dot_general(a, b, dims, preferred_element_type=F32)


def factor_of(keep, exps):
    return keep.astype(F32) * (jnp.left_shift(1, exps + 1).astype(F32) * 0.5)


def scale_kernel(kg, ku, kd, eg, eu, ed, gate, up, down, pair_out, down_out, pair_mask, down_mask):
    i = pl.program_id(0)
    cols = gate.shape[1] // BLOCK
    for j in range(cols):
        at = pl.ds(j * BLOCK, BLOCK)
        there = pl.ds((cols + j) * BLOCK, BLOCK)
        gate_factor = jnp.full((BLOCK, BLOCK), factor_of(kg[i, j], eg[i, j]), F32).astype(BF16)
        up_factor = jnp.full((BLOCK, BLOCK), factor_of(ku[i, j], eu[i, j]), F32).astype(BF16)
        down_factor = jnp.full((BLOCK, BLOCK), factor_of(kd[i, j], ed[i, j]), F32).astype(BF16)
        pair_mask[:, at] = gate_factor
        pair_mask[:, there] = up_factor
        down_mask[at, :] = down_factor
        pair_out[:, at] = gate[:, at] * gate_factor
        pair_out[:, there] = up[:, at] * up_factor
        down_out[at, :] = down[at, :] * down_factor


def scale_weights(gate_w, up_w, down_w, keep_gate, keep_up, keep_down, exp_gate, exp_up, exp_down):
    panel, width = gate_w.shape
    smem = pl.BlockSpec(memory_space=pltpu.SMEM)
    wide = pl.BlockSpec((BLOCK, width), lambda i: (i, 0))
    pair = pl.BlockSpec((BLOCK, 2 * width), lambda i: (i, 0))
    tall = pl.BlockSpec((width, BLOCK), lambda i: (0, i))
    pair_shape = jax.ShapeDtypeStruct((panel, 2 * width), BF16)
    down_shape = jax.ShapeDtypeStruct((width, panel), BF16)
    return pl.pallas_call(
        scale_kernel,
        grid=(panel // BLOCK,),
        in_specs=[smem] * 6 + [wide, wide, tall],
        out_specs=[pair, tall, pair, tall],
        out_shape=[pair_shape, down_shape, pair_shape, down_shape],
        compiler_params=pltpu.CompilerParams(vmem_limit_bytes=6 * 2**20),
        name="scale_weights",
    )(keep_gate, keep_up, keep_down.T, exp_gate, exp_up, exp_down.T, gate_w, up_w, down_w)


def activate(gate, up, hidden_grad):
    sig = jax.nn.sigmoid(gate)
    hidden = (gate * sig * up).astype(BF16)
    gate_grad = (hidden_grad * up * sig * (1.0 + gate * (1.0 - sig))).astype(BF16)
    up_grad = (hidden_grad * gate * sig).astype(BF16)
    return (hidden, gate_grad, up_grad)


def shift(x, first, k):
    pairs = []
    for row in range(16):
        for col in range(4):
            for depth in range(4):
                if (row % 2 == 0) == first:
                    there = (row * 4 + col) * 4 + (depth + k) % 4
                else:
                    there = (row * 4 + (col + k) % 4) * 4 + depth
                pairs.append(((row * 4 + col) * 4 + depth, there))
    return lax.ppermute(x, ("row", "col", "depth"), pairs)


def zshift(x, k):
    return lax.ppermute(x, "row", [(i, (i + 2 * k) % 16) for i in range(16)])


def swap_core(x):
    return lax.ppermute(x, "row", [(i, i ^ 1) for i in range(16)])


def pick(x, index, axis=0):
    return lax.dynamic_index_in_dim(x, index, axis, keepdims=False)


def put(x, block, index, axis=0):
    return lax.dynamic_update_index_in_dim(x, block, index, axis)


def zero_after(x):
    x = lax.slice(x, (0,) * x.ndim, (1,) * x.ndim).reshape(())
    return (x != x).astype(jnp.int32)


def place(core, col, depth, k, j):
    along_depth = (col + j) % 4 * 4 + (depth + k) % 4
    along_col = (col + k) % 4 * 4 + (depth + j) % 4
    return jnp.where(core == 0, along_depth, along_col ^ 8)


def gather_xy_first(block):
    return [block] + [shift(block, True, k) for k in range(1, 4)]


def gather_xy_second(got, core, col, depth):
    block = got[0]
    got = jnp.stack(got)
    whole = jnp.zeros((16, *block.shape), block.dtype)
    for j in (0, 1, 3, 2):
        came = got if j == 0 else shift(got, False, j)
        for k in range(4):
            whole = put(whole, came[k], place(core, col, depth, -k, -j))
    return whole.reshape(-1, block.shape[1])


def sum_over_xy(term, core, col, depth):
    width = term.shape[1]
    parts = term.reshape(16, -1, width)
    part = None
    for k in (1, 3, 2, 0):
        block = jnp.stack([pick(parts, place(core, col, depth, j, k)) for j in range(4)])
        block = (block if k == 0 else shift(block, False, k)).astype(F32)
        part = block if part is None else part + block
    part16 = part.astype(BF16)
    total = part[0]
    for j in (1, 3, 2):
        total += shift(part16[j], True, j).astype(F32)
    return total


def sum_over_z(mine, z):
    ahead = mine((z + 4) % 8)
    back = mine((z - 3) % 8)
    for s in range(4):
        ahead = zshift(ahead, 1)
        if s < 3:
            ahead = add16(ahead, mine((z + 3 - s) % 8))
            back = zshift(back, -1)
            if s < 2:
                back = add16(back, mine((z - 2 + s) % 8))
    return mine(z).astype(F32) + ahead.astype(F32) + back.astype(F32)


def gather_z(block, z):
    rows, width = block.shape
    whole = put(jnp.zeros((8, rows, width), block.dtype), block, z)
    ahead, back = block, block
    for s in range(4):
        ahead = zshift(ahead, 1)
        whole = put(whole, ahead, (z - 1 - s) % 8)
        if s < 3:
            back = zshift(back, -1)
            whole = put(whole, back, (z + 1 + s) % 8)
    return whole.reshape(8 * rows, width)


def add16(a, b):
    return (a.astype(F32) + b.astype(F32)).astype(F16)


def back_kernel(*refs):
    *acts, pair, down, out = refs
    width, panel = down.shape
    rows = acts[0].shape[0]
    for i, act in enumerate(acts):
        at = pl.ds(i * rows, rows)
        out[at, pl.ds(0, panel)] = dot(act[:, pl.ds(0, width)], down[...]).astype(BF16)
        out[at, pl.ds(panel, panel)] = dot(act[:, pl.ds(width, 2 * width)], pair[...], NT).astype(BF16)


def back_terms(acts, paired, eff_down):
    panel = eff_down.shape[1]
    rows = sum(a.shape[0] for a in acts)
    flops = 2 * rows * panel * 3 * eff_down.shape[0]
    return pl.pallas_call(
        back_kernel,
        in_specs=[pl.BlockSpec(memory_space=pltpu.VMEM)] * (len(acts) + 2),
        out_specs=pl.BlockSpec(memory_space=pltpu.VMEM),
        out_shape=jax.ShapeDtypeStruct((rows, 2 * panel), BF16),
        cost_estimate=pl.CostEstimate(flops=flops, bytes_accessed=12 * 2**20, transcendentals=0),
        compiler_params=pltpu.CompilerParams(vmem_limit_bytes=14 * 2**20),
        name="back_terms",
    )(*acts, paired, eff_down)


def shards(
    tokens,
    out_grad,
    gate_w,
    up_w,
    down_w,
    keep_gate,
    keep_up,
    keep_down,
    exp_gate,
    exp_up,
    exp_down,
):
    row = lax.axis_index("row")
    z, core = row // 2, row % 2
    col, depth = lax.axis_index("col"), lax.axis_index("depth")
    width = gate_w.shape[1]
    panel = gate_w.shape[0]

    got = gather_xy_first(jnp.concatenate([tokens, out_grad], axis=1))
    paired, eff_down, pair_mask, down_mask = scale_weights(
        gate_w, up_w, down_w, keep_gate, keep_up, keep_down, exp_gate + zero_after(got[3]), exp_up, exp_down
    )
    gathered = gather_xy_second(got, core, col, depth)
    half = gathered.shape[0] // 2
    rows = half // STREAMS

    def pair_term(at):
        return dot(gathered[at : at + rows, :panel], paired) * PAIR_SCALE

    def grad_term(at):
        return dot(gathered[at : at + rows, panel:], eff_down, NT) * GRAD_SCALE

    came, acts = [], []
    for s in range(STREAMS):
        at = half + s * rows
        came.append((swap_core(pair_term(at).astype(F16)), swap_core(grad_term(at).astype(F16))))
    for s in range(STREAMS):
        mine_pair = (pair_term(s * rows) + came[s][0].astype(F32)).astype(F16)
        mine_grad = (grad_term(s * rows) + came[s][1].astype(F32)).astype(F16)
        mine_pair = mine_pair.reshape(8, -1, 2 * width)
        mine_grad = mine_grad.reshape(8, -1, width)

        def mine(at, a=mine_pair, b=mine_grad):
            return jnp.concatenate([pick(a, at), pick(b, at)], axis=1)

        sums = sum_over_z(mine, z)
        act = activate(
            sums[:, :width] * (1.0 / PAIR_SCALE),
            sums[:, width : 2 * width] * (1.0 / PAIR_SCALE),
            sums[:, 2 * width :] * (1.0 / GRAD_SCALE),
        )
        acts.append(gather_z(jnp.concatenate(act, axis=1), z))
    acts += [swap_core(a) for a in acts]
    result = sum_over_xy(back_terms(acts, paired, eff_down), core, col, depth).astype(BF16)
    output, input_grad = result[:, :panel], result[:, panel:]

    all_tokens, all_grads = gathered[:, :panel], gathered[:, panel:]
    whole = jnp.concatenate(acts)
    hidden_all, pair_grad = whole[:, :width], whole[:, width:]

    down_w_grad = (dot(hidden_all, all_grads, TN) * down_mask.astype(F32)).astype(BF16)
    gate_w_grad = (
        dot(all_tokens, pair_grad[:, :width], TN) * pair_mask[:, :width].astype(F32)
    ).astype(BF16)
    up_w_grad = (
        dot(all_tokens, pair_grad[:, width:], TN) * pair_mask[:, width:].astype(F32)
    ).astype(BF16)
    return (output, input_grad, gate_w_grad, up_w_grad, down_w_grad)


def solution(mesh):
    act = P(("col", "depth"), "row")
    wide = P("row", ("col", "depth"))
    return jax.shard_map(
        shards,
        mesh=mesh,
        in_specs=(act, act, wide, wide, act, wide, wide, act, wide, wide, act),
        out_specs=(act, act, wide, wide, act),
        check_vma=False,
    )
```

```python
import jax
import jax.numpy as jnp
from jax import lax
from jax.experimental import pallas as pl
from jax.experimental.pallas import tpu as pltpu
from jax.sharding import PartitionSpec as P

F32 = jnp.float32
BF16 = jnp.bfloat16
F16 = jnp.float16
BLOCK = 128
STREAMS = 2

PAIR_SCALE = 4.0
GRAD_SCALE = 8.0

NT = (((1,), (1,)), ((), ()))
TN = (((0,), (0,)), ((), ()))


def dot(a, b, dims=(((1,), (0,)), ((), ()))):
    return lax.dot_general(a, b, dims, preferred_element_type=F32)


def factor_of(keep, exps):
    return keep.astype(F32) * (jnp.left_shift(1, exps + 1).astype(F32) * 0.5)


def scale_kernel(kg, ku, kd, eg, eu, ed, gate, up, down, pair_out, down_out, pair_mask, down_mask):
    i = pl.program_id(0)
    cols = gate.shape[1] // BLOCK
    for j in range(cols):
        at = pl.ds(j * BLOCK, BLOCK)
        there = pl.ds((cols + j) * BLOCK, BLOCK)
        gate_factor = jnp.full((BLOCK, BLOCK), factor_of(kg[i, j], eg[i, j]), F32).astype(BF16)
        up_factor = jnp.full((BLOCK, BLOCK), factor_of(ku[i, j], eu[i, j]), F32).astype(BF16)
        down_factor = jnp.full((BLOCK, BLOCK), factor_of(kd[i, j], ed[i, j]), F32).astype(BF16)
        pair_mask[:, at] = gate_factor
        pair_mask[:, there] = up_factor
        down_mask[at, :] = down_factor
        pair_out[:, at] = gate[:, at] * gate_factor
        pair_out[:, there] = up[:, at] * up_factor
        down_out[at, :] = down[at, :] * down_factor


def scale_weights(gate_w, up_w, down_w, keep_gate, keep_up, keep_down, exp_gate, exp_up, exp_down):
    panel, width = gate_w.shape
    smem = pl.BlockSpec(memory_space=pltpu.SMEM)
    wide = pl.BlockSpec((BLOCK, width), lambda i: (i, 0))
    pair = pl.BlockSpec((BLOCK, 2 * width), lambda i: (i, 0))
    tall = pl.BlockSpec((width, BLOCK), lambda i: (0, i))
    pair_shape = jax.ShapeDtypeStruct((panel, 2 * width), BF16)
    down_shape = jax.ShapeDtypeStruct((width, panel), BF16)
    return pl.pallas_call(
        scale_kernel,
        grid=(panel // BLOCK,),
        in_specs=[smem] * 6 + [wide, wide, tall],
        out_specs=[pair, tall, pair, tall],
        out_shape=[pair_shape, down_shape, pair_shape, down_shape],
        compiler_params=pltpu.CompilerParams(vmem_limit_bytes=6 * 2**20),
        name="scale_weights",
    )(keep_gate, keep_up, keep_down.T, exp_gate, exp_up, exp_down.T, gate_w, up_w, down_w)


def activate(gate, up, hidden_grad):
    sig = jax.nn.sigmoid(gate)
    hidden = (gate * sig * up).astype(BF16)
    gate_grad = (hidden_grad * up * sig * (1.0 + gate * (1.0 - sig))).astype(BF16)
    up_grad = (hidden_grad * gate * sig).astype(BF16)
    return (hidden, gate_grad, up_grad)


def shift(x, first, k):
    pairs = []
    for row in range(16):
        for col in range(4):
            for depth in range(4):
                if (row % 2 == 0) == first:
                    there = (row * 4 + col) * 4 + (depth + k) % 4
                else:
                    there = (row * 4 + (col + k) % 4) * 4 + depth
                pairs.append(((row * 4 + col) * 4 + depth, there))
    return lax.ppermute(x, ("row", "col", "depth"), pairs)


def zshift(x, k):
    return lax.ppermute(x, "row", [(i, (i + 2 * k) % 16) for i in range(16)])


def swap_core(x):
    return lax.ppermute(x, "row", [(i, i ^ 1) for i in range(16)])


def pick(x, index, axis=0):
    return lax.dynamic_index_in_dim(x, index, axis, keepdims=False)


def put(x, block, index, axis=0):
    return lax.dynamic_update_index_in_dim(x, block, index, axis)


def zero_after(x):
    x = lax.slice(x, (0,) * x.ndim, (1,) * x.ndim).reshape(())
    return (x != x).astype(jnp.int32)


def place(core, col, depth, k, j):
    along_depth = (col + j) % 4 * 4 + (depth + k) % 4
    along_col = (col + k) % 4 * 4 + (depth + j) % 4
    return jnp.where(core == 0, along_depth, along_col ^ 8)


def gather_xy_first(block):
    return [block] + [shift(block, True, k) for k in range(1, 4)]


def gather_xy_second(got, core, col, depth):
    block = got[0]
    got = jnp.stack(got)
    whole = jnp.zeros((16, *block.shape), block.dtype)
    for j in (0, 1, 3, 2):
        came = got if j == 0 else shift(got, False, j)
        for k in range(4):
            whole = put(whole, came[k], place(core, col, depth, -k, -j))
    return whole.reshape(-1, block.shape[1])


def sum_over_xy(term, core, col, depth):
    width = term.shape[1]
    parts = term.reshape(16, -1, width)
    part = None
    for k in (1, 3, 2, 0):
        block = jnp.stack([pick(parts, place(core, col, depth, j, k)) for j in range(4)])
        block = (block if k == 0 else shift(block, False, k)).astype(F32)
        part = block if part is None else part + block
    part16 = part.astype(BF16)
    total = part[0]
    for j in (1, 3, 2):
        total += shift(part16[j], True, j).astype(F32)
    return total


def sum_over_z(mine, z):
    ahead = mine((z + 4) % 8)
    back = mine((z - 3) % 8)
    for s in range(4):
        ahead = zshift(ahead, 1)
        if s < 3:
            ahead = add16(ahead, mine((z + 3 - s) % 8))
            back = zshift(back, -1)
            if s < 2:
                back = add16(back, mine((z - 2 + s) % 8))
    return mine(z).astype(F32) + ahead.astype(F32) + back.astype(F32)


def gather_z(block, z):
    rows, width = block.shape
    whole = put(jnp.zeros((8, rows, width), block.dtype), block, z)
    ahead, back = block, block
    for s in range(4):
        ahead = zshift(ahead, 1)
        whole = put(whole, ahead, (z - 1 - s) % 8)
        if s < 3:
            back = zshift(back, -1)
            whole = put(whole, back, (z + 1 + s) % 8)
    return whole.reshape(8 * rows, width)


def add16(a, b):
    return (a.astype(F32) + b.astype(F32)).astype(F16)


def back_kernel(*refs):
    pair, down, *acts = refs[:4]
    out = refs[-1]
    width, panel = down.shape
    rows = acts[0].shape[0]
    for i, act in enumerate(acts):
        at = pl.ds(i * rows, rows)
        out[at, pl.ds(0, panel)] = dot(act[:, pl.ds(0, width)], down[...]).astype(BF16)
        out[at, pl.ds(panel, panel)] = dot(act[:, pl.ds(width, 2 * width)], pair[...], NT).astype(BF16)


def back_terms(acts, paired, eff_down, part, into):
    panel = eff_down.shape[1]
    rows = sum(a.shape[0] for a in acts)
    given = [] if into is None else [into]
    return pl.pallas_call(
        back_kernel,
        grid=(1,),
        in_specs=[pl.BlockSpec(memory_space=pltpu.VMEM)] * 4 + [pl.BlockSpec(memory_space=pl.ANY)] * len(given),
        out_specs=pl.BlockSpec((rows, 2 * panel), lambda i: (part, 0)),
        out_shape=jax.ShapeDtypeStruct((2 * rows, 2 * panel), BF16),
        input_output_aliases={4: 0} if given else {},
        cost_estimate=pl.CostEstimate(
            flops=6 * rows * panel * eff_down.shape[0], bytes_accessed=6 * 2**20, transcendentals=0
        ),
        compiler_params=pltpu.CompilerParams(vmem_limit_bytes=6 * 2**20),
        name="back_terms",
    )(paired, eff_down, *acts, *given)


def shards(
    tokens,
    out_grad,
    gate_w,
    up_w,
    down_w,
    keep_gate,
    keep_up,
    keep_down,
    exp_gate,
    exp_up,
    exp_down,
):
    row = lax.axis_index("row")
    z, core = row // 2, row % 2
    col, depth = lax.axis_index("col"), lax.axis_index("depth")
    width = gate_w.shape[1]
    panel = gate_w.shape[0]

    got = gather_xy_first(jnp.concatenate([tokens, out_grad], axis=1))
    paired, eff_down, pair_mask, down_mask = scale_weights(
        gate_w, up_w, down_w, keep_gate, keep_up, keep_down, exp_gate + zero_after(got[3]), exp_up, exp_down
    )
    gathered = gather_xy_second(got, core, col, depth)
    half = gathered.shape[0] // 2
    rows = half // STREAMS

    def pair_term(at):
        return dot(gathered[at : at + rows, :panel], paired) * PAIR_SCALE

    def grad_term(at):
        return dot(gathered[at : at + rows, panel:], eff_down, NT) * GRAD_SCALE

    came, acts = [], []
    for s in range(STREAMS):
        at = half + s * rows
        came.append((swap_core(pair_term(at).astype(F16)), swap_core(grad_term(at).astype(F16))))
    for s in range(STREAMS):
        mine_pair = (pair_term(s * rows) + came[s][0].astype(F32)).astype(F16)
        mine_grad = (grad_term(s * rows) + came[s][1].astype(F32)).astype(F16)
        mine_pair = mine_pair.reshape(8, -1, 2 * width)
        mine_grad = mine_grad.reshape(8, -1, width)

        def mine(at, a=mine_pair, b=mine_grad):
            return jnp.concatenate([pick(a, at), pick(b, at)], axis=1)

        sums = sum_over_z(mine, z)
        act = activate(
            sums[:, :width] * (1.0 / PAIR_SCALE),
            sums[:, width : 2 * width] * (1.0 / PAIR_SCALE),
            sums[:, 2 * width :] * (1.0 / GRAD_SCALE),
        )
        acts.append(gather_z(jnp.concatenate(act, axis=1), z))
    others = [swap_core(a) for a in acts]
    back = back_terms(acts, paired, eff_down, 0, None)
    back = back_terms(others, paired, eff_down, 1, back)
    acts += others
    result = sum_over_xy(back, core, col, depth).astype(BF16)
    output, input_grad = result[:, :panel], result[:, panel:]

    all_tokens, all_grads = gathered[:, :panel], gathered[:, panel:]
    whole = jnp.concatenate(acts)
    hidden_all, pair_grad = whole[:, :width], whole[:, width:]

    down_w_grad = (dot(hidden_all, all_grads, TN) * down_mask.astype(F32)).astype(BF16)
    gate_w_grad = (
        dot(all_tokens, pair_grad[:, :width], TN) * pair_mask[:, :width].astype(F32)
    ).astype(BF16)
    up_w_grad = (
        dot(all_tokens, pair_grad[:, width:], TN) * pair_mask[:, width:].astype(F32)
    ).astype(BF16)
    return (output, input_grad, gate_w_grad, up_w_grad, down_w_grad)


def solution(mesh):
    act = P(("col", "depth"), "row")
    wide = P("row", ("col", "depth"))
    return jax.shard_map(
        shards,
        mesh=mesh,
        in_specs=(act, act, wide, wide, act, wide, wide, act, wide, wide, act),
        out_specs=(act, act, wide, wide, act),
        check_vma=False,
    )
```
